512 devices in a mesh: row: 32 (over y, x_hi, core), col: 16 (over x_lo, z).
Axes of the slice: x: 4 (x_hi: 2, x_lo: 2; x = x_hi * 2 + x_lo), y: 8, z: 8, core: 2. Of those that a mesh axis runs over, the one named last changes fastest.
Arguments:
- positions: int32 [32, 16, 2, 2], P('row', 'col'), may hold values from 0 to 255, as said below
- measured: bfloat16 [32, 16, 2, 256, 256], P('row', 'col'), may hold values from 0.099609375 to 3
- object_field: float32 [2, 8192, 4096], P(None, 'row', 'col'), may hold values from -5 to 5
- probe: float32 [2, 256, 256], replicated, may hold values from -5 to 5
Outputs:
- new_object: float32 [2, 8192, 4096], P(None, 'row', 'col')
- new_probe: float32 [2, 256, 256], replicated
The draws below stay inside these ranges and needn't reach their ends.
Inputs may be any that keep to these rules, and one draw needn't show every extreme that they name: `positions`: row offsets lie below 256 and column offsets below 256; the first position of the first tile sits at (255, 255) and the last position of the last tile at (0, 0).
All inputs are finite; a program needn't handle non-finite values.
Results may differ from the reference program's by a relative error of at most 0.0003.
Values sent between devices are 32-bit elements; how exact they have to be, the bound alone decides.
No kernel may reach another device: no remote copies, remote signals or barrier semaphores. Data moves between devices by JAX's collectives and lax.ppermute only.
A program may use at most 192 MiB of HBM per device.

```python
import math
import jax
import jax.numpy as jnp
from jax import lax

P_SIZE = 256
TILE_R = 256
TILE_C = 256
OWN = 2
ROW_TILES = 32
COL_TILES = 16
OBJ_R = 8192
OBJ_C = 4096


def draw_positions(key, part):
    key = jax.random.fold_in(key, 11)
    key_rows, key_cols = jax.random.split(key)
    row_draw = jax.random.randint(key_rows, (ROW_TILES, COL_TILES, OWN), 0, TILE_R)
    col_draw = jax.random.randint(key_cols, (ROW_TILES, COL_TILES, OWN), 0, TILE_C)
    offsets = jnp.stack([row_draw, col_draw], -1).astype(jnp.int32)
    offsets = offsets.at[0, 0, 0].set(jnp.array([TILE_R - 1, TILE_C - 1], jnp.int32))
    offsets = offsets.at[ROW_TILES - 1, COL_TILES - 1, OWN - 1].set(jnp.array([0, 0], jnp.int32))
    return offsets


def shard_levels(rng, extent, shards, least, high):
    def one(position, shards_of):
        draws = jax.random.uniform(jax.random.fold_in(jax.random.fold_in(rng, 6), position), (shards_of,), jnp.float32, least / len(shards), high / len(shards))
        return jnp.repeat(jnp.exp(draws), extent[position] // shards_of).reshape((-1,) + (1,) * (len(extent) - position - 1))

    gain = one(*shards[0])
    for cut in shards[1:]:
        gain = gain * one(*cut)
    return gain


def normal_values(stream_key, dims, width, limit, cuts=(), kind=jnp.bfloat16):
    result = width * jax.random.normal(stream_key, dims, jnp.float32)
    if cuts:
        result = result * shard_levels(stream_key, dims, cuts, -0.22, 0.18)
    return jnp.clip(result, -limit, limit).astype(kind)


def setup_inputs(seed: int = 0) -> dict:
    splits = jax.random.split(jax.random.key(seed), 5)
    positions = draw_positions(jax.random.fold_in(splits[4], 71), 0)
    measured = jnp.clip(jnp.exp(math.log(3.0) - 3.4051113 * jax.random.uniform(splits[1], (ROW_TILES, COL_TILES, OWN, P_SIZE, P_SIZE), jnp.float32) ** shard_levels(splits[1], (ROW_TILES, COL_TILES, OWN, P_SIZE, P_SIZE), ((0, 32), (1, 16)), -0.2, 0.2)), 0.099609375, 3.0).astype(jnp.bfloat16)
    object_field = normal_values(splits[2], (2, OBJ_R, OBJ_C), 0.7, 5.0, ((1, 32), (2, 16)), jnp.float32)
    probe = normal_values(splits[3], (2, P_SIZE, P_SIZE), 0.7, 5.0, (), jnp.float32)
    return dict(positions=positions, measured=measured, object_field=object_field, probe=probe)


def reference(positions, measured, object_field, probe):
    padded = jnp.pad(object_field, ((0, 0), (0, P_SIZE), (0, P_SIZE)))
    probe_wave = lax.complex(probe[0], probe[1])
    lighting = probe[0] * probe[0] + probe[1] * probe[1]
    zero = jnp.zeros((), jnp.int32)

    def tile_step(carry, tile_index):
        gradient, numerator, weight = carry
        tile_row = tile_index // COL_TILES
        tile_col = tile_index % COL_TILES
        row_start = (tile_row * TILE_R).astype(jnp.int32)
        col_start = (tile_col * TILE_C).astype(jnp.int32)
        window = lax.dynamic_slice(padded, (zero, row_start, col_start), (2, TILE_R + P_SIZE, TILE_C + P_SIZE))
        offsets = positions[tile_row, tile_col]
        amplitude = measured[tile_row, tile_col].astype(jnp.float32)
        patches = jax.vmap(lambda spot: lax.dynamic_slice(window, (zero, spot[0], spot[1]), (2, P_SIZE, P_SIZE)))(offsets)
        patch_wave = lax.complex(patches[:, 0], patches[:, 1])
        far_field = jnp.fft.fft2(probe_wave * patch_wave, norm='ortho')
        real_part = jnp.real(far_field)
        imag_part = jnp.imag(far_field)
        modulus = jnp.sqrt(jnp.maximum(real_part * real_part + imag_part * imag_part, 0.25))
        chi_wave = jnp.fft.ifft2(far_field * (amplitude / modulus) - far_field, norm='ortho')
        object_term = jnp.conj(probe_wave) * chi_wave
        probe_term = jnp.conj(patch_wave) * chi_wave
        numerator = numerator + jnp.stack([lax.optimization_barrier(jnp.sum(jnp.real(probe_term), 0)), lax.optimization_barrier(jnp.sum(jnp.imag(probe_term), 0))])
        weight = weight + lax.optimization_barrier(jnp.sum(patches[:, 0] * patches[:, 0] + patches[:, 1] * patches[:, 1], 0))
        terms = jnp.stack([jnp.real(object_term), jnp.imag(object_term), jnp.broadcast_to(lighting, object_term.shape)], 1)

        def place(member, local):
            spot = offsets[member]
            current = lax.dynamic_slice(local, (zero, spot[0], spot[1]), (3, P_SIZE, P_SIZE))
            return lax.dynamic_update_slice(local, current + terms[member], (zero, spot[0], spot[1]))
        local = lax.fori_loop(0, OWN, place, jnp.zeros((3, TILE_R + P_SIZE, TILE_C + P_SIZE), jnp.float32))
        current = lax.dynamic_slice(gradient, (zero, row_start, col_start), (3, TILE_R + P_SIZE, TILE_C + P_SIZE))
        gradient = lax.dynamic_update_slice(gradient, current + local, (zero, row_start, col_start))
        return ((gradient, numerator, weight), None)
    start = (jnp.zeros((3, OBJ_R + P_SIZE, OBJ_C + P_SIZE), jnp.float32), jnp.zeros((2, P_SIZE, P_SIZE), jnp.float32), jnp.zeros((P_SIZE, P_SIZE), jnp.float32))
    (gradient, numerator, weight), _ = lax.scan(tile_step, start, jnp.arange(ROW_TILES * COL_TILES, dtype=jnp.int32))
    gradient = gradient[:, :OBJ_R, :OBJ_C]
    new_object = object_field + gradient[:2] / (gradient[2] + 1.0)
    new_probe = probe + numerator / (weight + 1.0)
    return (new_object, new_probe)
```

```python
import functools
import math

import jax
import jax.numpy as jnp
import ml_dtypes
import numpy as np
from jax import lax
from jax.experimental import pallas as pl
from jax.experimental.pallas import tpu as pltpu
from jax.sharding import Mesh
from jax.sharding import PartitionSpec as P

SIDE = 256
ROW = ("y", "xh", "c")
COL = ("xl", "z")
PLANE = ("y", "xh", "xl")


def passed_along(value, axis, steps):
    count = lax.axis_size(axis)
    leading, last = (max(0, -steps), min(count, count - steps))
    return lax.ppermute(value, axis, [(source, source + steps) for source in range(leading, last)])


def dft_tables():
    indices = np.arange(SIDE)
    angles = (indices[:, None] * indices[None, :] % SIDE) * (2.0 * math.pi / SIDE)
    cosine = np.cos(angles) / math.sqrt(SIDE)
    sine = np.sin(angles) / math.sqrt(SIDE)
    forward = np.block([[cosine, sine], [-sine, cosine]])
    both = np.stack([forward, forward.T])
    head = both.astype(ml_dtypes.bfloat16)
    rest = (both - head.astype(np.float64)).astype(ml_dtypes.bfloat16)
    return np.stack([head, rest], 1)


def halves(value):
    head = value.astype(jnp.bfloat16)
    return head, (value - head.astype(jnp.float32)).astype(jnp.bfloat16)


def dot(left, right):
    return jnp.dot(left, right, preferred_element_type=jnp.float32)


def apply_left(tables, which, value):
    head, rest = halves(value)
    return dot(tables[which, 0], head) + dot(tables[which, 0], rest) + dot(tables[which, 1], head)


def apply_right(tables, which, value):
    head, rest = halves(value)
    return dot(head, tables[which, 0]) + dot(rest, tables[which, 0]) + dot(head, tables[which, 1])


def rolled(value, rows, cols):
    return pltpu.roll(pltpu.roll(value, rows, 0), cols, 1)


def quadrants(row, col):
    below = lax.broadcasted_iota(jnp.int32, (SIDE, SIDE), 0) < row
    right = lax.broadcasted_iota(jnp.int32, (SIDE, SIDE), 1) < col
    return below, right


def prepare_kernel(own, left, upper, corner, probe, rolled_probe, lighting):
    total = jnp.ones((SIDE, SIDE), jnp.float32)
    for k in range(2):
        row, col = own[k, 0], own[k, 1]
        real = rolled(probe[0], row, col)
        imag = rolled(probe[1], row, col)
        rolled_probe[k, 0] = real
        rolled_probe[k, 1] = imag
        below, right = quadrants(row, col)
        total += jnp.where(below | right, 0.0, real * real + imag * imag)
    intensity = probe[0] * probe[0] + probe[1] * probe[1]
    for k in range(2):
        for spots, lies_below, lies_right in ((left, False, True), (upper, True, False), (corner, True, True)):
            row, col = spots[k, 0], spots[k, 1]
            below, right = quadrants(row, col)
            inside = (below == lies_below) & (right == lies_right)
            total += jnp.where(inside, rolled(intensity, row, col), 0.0)
    lighting[...] = total


def visit_kernel(
    own, core, tile, right_tile, below_tile, corner_tile, rolled_probe, amplitude, tables,
    step_own, step_right, step_row, kept, sent, patches,
):
    exits = []
    for k in range(2):
        below, right = quadrants(own[k, 0], own[k, 1])
        for part in range(2):
            patches[k, part] = jnp.where(
                below,
                jnp.where(right, corner_tile[part], below_tile[part]),
                jnp.where(right, right_tile[part], tile[part]),
            )
        pr, pi = rolled_probe[k, 0], rolled_probe[k, 1]
        qr, qi = patches[k, 0], patches[k, 1]
        exits.append(jnp.concatenate([pr * qr - pi * qi, pr * qi + pi * qr], 0))
    field = apply_left(tables, 0, jnp.concatenate(exits, 1))
    field = jnp.concatenate(
        [jnp.concatenate([field[:SIDE, k * SIDE : (k + 1) * SIDE], field[SIDE:, k * SIDE : (k + 1) * SIDE]], 1) for k in range(2)], 0
    )
    far = apply_right(tables, 1, field)
    far_real, far_imag = far[:, :SIDE], far[:, SIDE:]
    power = jnp.maximum(far_real * far_real + far_imag * far_imag, 0.25)
    factor = amplitude[...].reshape(2 * SIDE, SIDE).astype(jnp.float32) * lax.rsqrt(power) - 1.0
    change_real, change_imag = far_real * factor, far_imag * factor
    change = jnp.concatenate(
        [jnp.concatenate([change_real[k * SIDE : (k + 1) * SIDE], change_imag[k * SIDE : (k + 1) * SIDE]], 0) for k in range(2)], 1
    )
    field = apply_left(tables, 1, change)
    field = jnp.concatenate(
        [jnp.concatenate([field[:SIDE, k * SIDE : (k + 1) * SIDE], field[SIDE:, k * SIDE : (k + 1) * SIDE]], 1) for k in range(2)], 0
    )
    chi = apply_right(tables, 0, field)
    numerator = [jnp.zeros((SIDE, SIDE), jnp.float32)] * 3
    steps = [[jnp.zeros((SIDE, SIDE), jnp.float32)] * 4 for _ in range(2)]
    for k in range(2):
        row, col = own[k, 0], own[k, 1]
        below, right = quadrants(row, col)
        chi_real = chi[k * SIDE : (k + 1) * SIDE, :SIDE]
        chi_imag = chi[k * SIDE : (k + 1) * SIDE, SIDE:]
        pr, pi = rolled_probe[k, 0], rolled_probe[k, 1]
        qr, qi = patches[k, 0], patches[k, 1]
        back_row, back_col = (SIDE - row) & (SIDE - 1), (SIDE - col) & (SIDE - 1)
        terms = (qr * chi_real + qi * chi_imag, qr * chi_imag - qi * chi_real, qr * qr + qi * qi)
        numerator = [total + rolled(term, back_row, back_col) for total, term in zip(numerator, terms)]
        places = (
            jnp.logical_not(below | right),
            right & jnp.logical_not(below),
            below & jnp.logical_not(right),
            below & right,
        )
        for part, term in enumerate((pr * chi_real + pi * chi_imag, pr * chi_imag - pi * chi_real)):
            steps[part] = [total + jnp.where(place, term, 0.0) for total, place in zip(steps[part], places)]
    for part in range(2):
        step_own[part] = steps[part][0]
        step_right[part] = steps[part][1]
        step_row[0, part] = steps[part][2]
        step_row[1, part] = steps[part][3]
    first = core[0] == 0
    half = SIDE // 2
    for layer in range(3):
        one, other = numerator[layer][:, :half], numerator[layer][:, half:]
        kept[:, layer] = jnp.where(first, one, other).reshape(SIDE // 8, 8, half)
        sent[:, layer] = jnp.where(first, other, one).reshape(SIDE // 8, 8, half)


def vmem():
    return pl.BlockSpec(memory_space=pltpu.VMEM)


def smem():
    return pl.BlockSpec(memory_space=pltpu.SMEM)


def shape(*sizes):
    return jax.ShapeDtypeStruct(sizes, jnp.float32)


def prepare(own, left, upper, corner, probe):
    return pl.pallas_call(
        prepare_kernel,
        out_shape=(shape(2, 2, SIDE, SIDE), shape(SIDE, SIDE)),
        in_specs=[smem()] * 4 + [vmem()],
        out_specs=(vmem(), vmem()),
        cost_estimate=pl.CostEstimate(flops=4000000, bytes_accessed=4 << 20, transcendentals=0),
        compiler_params=pltpu.CompilerParams(vmem_limit_bytes=16 << 20),
    )(own, left, upper, corner, probe)


def visit(own, core, tile, right_tile, below_tile, corner_tile, rolled_probe, amplitude, tables):
    rows = SIDE // 8
    return pl.pallas_call(
        visit_kernel,
        out_shape=(
            shape(2, SIDE, SIDE),
            shape(2, SIDE, SIDE),
            shape(2, 2, SIDE, SIDE),
            shape(rows, 3, 8, SIDE // 2),
            shape(rows, 3, 8, SIDE // 2),
        ),
        in_specs=[smem(), smem()] + [vmem()] * 7,
        out_specs=(vmem(),) * 5,
        scratch_shapes=[pltpu.VMEM((2, 2, SIDE, SIDE), jnp.float32)],
        cost_estimate=pl.CostEstimate(flops=24 * 2 * 256**3 * 4, bytes_accessed=8 << 20, transcendentals=131072),
        compiler_params=pltpu.CompilerParams(vmem_limit_bytes=32 << 20),
    )(own, core, tile, right_tile, below_tile, corner_tile, rolled_probe, amplitude, tables)


def everywhere(value, axis):
    copies = jnp.broadcast_to(value[None], (lax.axis_size(axis),) + value.shape)
    return lax.all_to_all(copies, axis, 0, 0)


def body(positions, measured, object_field, probe):
    own = positions[0, 0]
    amplitude = measured[0, 0]
    right_tile = passed_along(object_field, COL, -1)
    below_tile = passed_along(object_field, ROW, -1)
    left = passed_along(own, COL, 1)
    upper = passed_along(own, ROW, 1)
    corner = passed_along(left, ROW, 1)
    corner_tile = passed_along(right_tile, ROW, -1)
    rolled_probe, lighting = prepare(own, left, upper, corner, probe)
    core = lax.axis_index("c")
    step_own, step_right, step_row, kept, sent = visit(
        own, core[None], object_field, right_tile, below_tile, corner_tile, rolled_probe, amplitude, jnp.asarray(dft_tables())
    )
    other = lax.ppermute(sent, "c", [(0, 1), (1, 0)])
    step_row = passed_along(step_row, ROW, 1)
    rows = SIDE // 8
    summed = lax.all_to_all((kept + other).reshape(rows, 24, SIDE // 2), PLANE, 0, 0).sum(0)
    step_right = passed_along(step_right + step_row[1], COL, 1)
    summed = everywhere(summed, "z").sum(0).reshape(3, 8, SIDE // 2)
    place = lax.axis_index(PLANE)
    mine = lax.dynamic_slice(probe, (0, place * 8, core * (SIDE // 2)), (2, 8, SIDE // 2))
    mine = mine + summed[:2] / (summed[2] + 1.0)
    near = everywhere(mine.reshape(16, SIDE // 2), PLANE)
    far = lax.ppermute(near, "c", [(0, 1), (1, 0)])
    pair = jnp.where(core == 0, jnp.stack([near, far]), jnp.stack([far, near]))
    new_probe = pair.reshape(2, rows, 2, 8, SIDE // 2).transpose(2, 1, 3, 0, 4).reshape(2, SIDE, SIDE)
    new_object = object_field + (step_own + step_row[0] + step_right) / lighting
    return (new_object, new_probe)


def solution(mesh):
    split = Mesh(mesh.devices.reshape(8, 2, 2, 2, 8), ROW + COL)
    in_specs = (P(ROW, COL), P(ROW, COL), P(None, ROW, COL), P())
    out_specs = (P(None, ROW, COL), P())
    return jax.shard_map(body, mesh=split, in_specs=in_specs, out_specs=out_specs, check_vma=False)
```

```python
import math

import jax
import jax.numpy as jnp
import ml_dtypes
import numpy as np
from jax import lax
from jax.experimental import pallas as pl
from jax.experimental.pallas import tpu as pltpu
from jax.sharding import Mesh
from jax.sharding import PartitionSpec as P

SIDE = 256
ROW = ("y", "xh", "c")
COL = ("xl", "z")
PLANE = ("xh", "xl", "z")


def passed_along(value, axis, steps):
    count = lax.axis_size(axis)
    leading, last = (max(0, -steps), min(count, count - steps))
    return lax.ppermute(value, axis, [(source, source + steps) for source in range(leading, last)])


def dft_tables():
    indices = np.arange(SIDE)
    angles = (indices[:, None] * indices[None, :] % SIDE) * (2.0 * math.pi / SIDE)
    cosine, sine = np.cos(angles) / math.sqrt(SIDE), np.sin(angles) / math.sqrt(SIDE)
    three = np.stack([cosine, sine, -sine])
    head = three.astype(ml_dtypes.bfloat16)
    rest = (three - head.astype(np.float64)).astype(ml_dtypes.bfloat16)
    return np.stack([head, rest], 1)


def halves(value):
    head = value.astype(jnp.bfloat16)
    return head, (value - head.astype(jnp.float32)).astype(jnp.bfloat16)


def dot(left, right):
    return jnp.dot(left, right, preferred_element_type=jnp.float32)


def block(tables, sign, which):
    up, down = (1, 2) if sign > 0 else (2, 1)
    upper = jnp.concatenate([tables[0, which], tables[up, which]], 1)
    return jnp.concatenate([upper, jnp.concatenate([tables[down, which], tables[0, which]], 1)], 0)


def apply_left(tables, sign, value):
    head, rest = halves(value)
    matrix = block(tables, sign, 0)
    return dot(matrix, head) + dot(matrix, rest) + dot(block(tables, sign, 1), head)


def apply_right(tables, sign, value):
    head, rest = halves(value)
    matrix = block(tables, sign, 0)
    return dot(head, matrix) + dot(rest, matrix) + dot(head, block(tables, sign, 1))


def to_columns(value):
    return jnp.concatenate(
        [jnp.concatenate([value[:SIDE, k * SIDE : (k + 1) * SIDE], value[SIDE:, k * SIDE : (k + 1) * SIDE]], 1) for k in range(2)], 0
    )


def rolled(value, rows, cols):
    return pltpu.roll(pltpu.roll(value, rows, 0), cols, 1)


def quadrants(row, col):
    below = lax.broadcasted_iota(jnp.int32, (SIDE, SIDE), 0) < row
    right = lax.broadcasted_iota(jnp.int32, (SIDE, SIDE), 1) < col
    return below, right


def prepare_kernel(own, probe, rolled_probe):
    for k in range(2):
        for part in range(2):
            rolled_probe[k, part] = rolled(probe[part], own[k, 0], own[k, 1])


def carried(block, first):
    line = lax.broadcasted_iota(jnp.int32, block.shape, 0)
    last = lax.broadcasted_iota(jnp.int32, block.shape, 1) == block.shape[1] - 1
    return [jnp.sum(jnp.where(last & (line == first + k), block, 0.0)).astype(jnp.int32) for k in range(4)]


def finish_kernel(own, probe, tile, step_own, step_row, step_right, new_tile):
    half = SIDE // 2
    intensity = probe[0] * probe[0] + probe[1] * probe[1]
    beside, above = step_right[0, :8, half:], step_row[1, 0, :8, half:]
    total = jnp.ones((SIDE, SIDE), jnp.float32)
    for spots, lies_below, lies_right in (
        ([own[k // 2, k % 2] for k in range(4)], False, False),
        (carried(beside, 4), False, True),
        (carried(above, 0), True, False),
        (carried(beside, 0), True, True),
    ):
        for k in range(2):
            row, col = spots[2 * k], spots[2 * k + 1]
            below, right = quadrants(row, col)
            inside = (below == lies_below) & (right == lies_right)
            total += jnp.where(inside, rolled(intensity, row, col), 0.0)
    last = lax.broadcasted_iota(jnp.int32, (SIDE, SIDE), 1) == SIDE - 1
    for part in range(2):
        arrived = step_row[0, part] + jnp.where(last, 0.0, step_right[part])
        new_tile[part] = tile[part] + (step_own[part] + arrived) / total


def visit_kernel(
    own, core, tile, right_real, right_imag, below_tile, corner_real, corner_imag, rolled_probe, amplitude,
    tables, kept, sent, step_own, step_right, step_row, patches, near_row, stored,
):
    right_tile, corner_tile = (right_real, right_imag), (corner_real, corner_imag)
    exits = []
    for k in range(2):
        below, right = quadrants(own[k, 0], own[k, 1])
        for part in range(2):
            patches[k, part] = jnp.where(
                below,
                jnp.where(right, corner_tile[part][...], below_tile[part]),
                jnp.where(right, right_tile[part][...], tile[part]),
            )
        pr, pi = rolled_probe[k, 0], rolled_probe[k, 1]
        qr, qi = patches[k, 0], patches[k, 1]
        exits.append(jnp.concatenate([pr * qr - pi * qi, pr * qi + pi * qr], 0))
    exits = jnp.concatenate(exits, 1)
    field = to_columns(apply_left(tables, 1, exits))
    far = apply_right(tables, -1, field)
    far_real, far_imag = far[:, :SIDE], far[:, SIDE:]
    power = jnp.maximum(far_real * far_real + far_imag * far_imag, 0.25)
    factor = amplitude[...].reshape(2 * SIDE, SIDE).astype(jnp.float32) * lax.rsqrt(power) - 1.0
    change_real, change_imag = far_real * factor, far_imag * factor
    change = jnp.concatenate(
        [jnp.concatenate([change_real[k * SIDE : (k + 1) * SIDE], change_imag[k * SIDE : (k + 1) * SIDE]], 0) for k in range(2)], 1
    )
    chi = apply_right(tables, 1, to_columns(apply_left(tables, -1, change)))
    numerator = [jnp.zeros((SIDE, SIDE), jnp.float32)] * 3
    for k in range(2):
        chi_real = chi[k * SIDE : (k + 1) * SIDE, :SIDE]
        chi_imag = chi[k * SIDE : (k + 1) * SIDE, SIDE:]
        qr, qi = patches[k, 0], patches[k, 1]
        back_row, back_col = (SIDE - own[k, 0]) & (SIDE - 1), (SIDE - own[k, 1]) & (SIDE - 1)
        terms = (qr * chi_real + qi * chi_imag, qr * chi_imag - qi * chi_real, qr * qr + qi * qi)
        numerator = [total + rolled(term, back_row, back_col) for total, term in zip(numerator, terms)]
    first = core[0] == 0
    half = SIDE // 2
    for layer in range(3):
        one, other = numerator[layer][:, :half], numerator[layer][:, half:]
        kept[:, layer] = jnp.where(first, one, other).reshape(SIDE // 8, 8, half)
        sent[:, layer] = jnp.where(first, other, one).reshape(SIDE // 8, 8, half)
    line = lax.broadcasted_iota(jnp.int32, (8, half), 0)
    last = lax.broadcasted_iota(jnp.int32, (8, half), 1) == half - 1
    spots = jnp.zeros((8, half), jnp.int32)
    for k in range(4):
        spots = jnp.where((line & 3) == k, own[k // 2, k % 2], spots)
    spots = spots.astype(jnp.float32)

    def step(part, inside):
        total = jnp.zeros((SIDE, SIDE), jnp.float32)
        for k in range(2):
            chi_real = chi[k * SIDE : (k + 1) * SIDE, :SIDE]
            chi_imag = chi[k * SIDE : (k + 1) * SIDE, SIDE:]
            pr, pi = rolled_probe[k, 0], rolled_probe[k, 1]
            term = pr * chi_imag - pi * chi_real if part else pr * chi_real + pi * chi_imag
            total += jnp.where(inside(*quadrants(own[k, 0], own[k, 1])), term, 0.0)
        return total

    for part in range(2):
        near_row[0, part] = step(part, lambda below, right: below & jnp.logical_not(right))
        near_row[1, part] = step(part, lambda below, right: below & right)
    near_row[1, 0, :8, half:] = jnp.where(last & (line < 4), spots, near_row[1, 0, :8, half:])
    store = pltpu.make_async_copy(near_row, step_row, stored)
    store.start()
    for part in range(2):
        step_right[part] = step(part, lambda below, right: right & jnp.logical_not(below))
        step_own[part] = step(part, lambda below, right: jnp.logical_not(below | right))
    step_right[0, :8, half:] = jnp.where(last & (line >= 4), spots, step_right[0, :8, half:])
    store.wait()


def vmem():
    return pl.BlockSpec(memory_space=pltpu.VMEM)


def smem():
    return pl.BlockSpec(memory_space=pltpu.SMEM)


def shape(*sizes):
    return jax.ShapeDtypeStruct(sizes, jnp.float32)


def anywhere():
    return pl.BlockSpec(memory_space=pl.ANY)


def prepare(own, probe):
    return pl.pallas_call(
        prepare_kernel,
        out_shape=shape(2, 2, SIDE, SIDE),
        in_specs=[smem(), vmem()],
        out_specs=vmem(),
        cost_estimate=pl.CostEstimate(flops=2000000, bytes_accessed=2 << 20, transcendentals=0),
        compiler_params=pltpu.CompilerParams(vmem_limit_bytes=16 << 20),
    )(own, probe)


def finish(own, probe, tile, step_own, step_row, step_right):
    return pl.pallas_call(
        finish_kernel,
        out_shape=shape(2, SIDE, SIDE),
        in_specs=[smem()] + [vmem()] * 5,
        out_specs=vmem(),
        cost_estimate=pl.CostEstimate(flops=8000000, bytes_accessed=8 << 20, transcendentals=0),
        compiler_params=pltpu.CompilerParams(vmem_limit_bytes=16 << 20),
    )(own, probe, tile, step_own, step_row, step_right)


def visit(own, core, tile, right_real, right_imag, below_tile, corner_real, corner_imag, rolled_probe, amplitude, tables):
    rows = SIDE // 8
    out_shape = (
        shape(rows, 3, 8, SIDE // 2),
        shape(rows, 3, 8, SIDE // 2),
        shape(2, SIDE, SIDE),
        shape(2, SIDE, SIDE),
        shape(2, 2, SIDE, SIDE),
    )
    return pl.pallas_call(
        visit_kernel,
        out_shape=out_shape,
        in_specs=[smem(), smem()] + [vmem()] * 9,
        out_specs=(vmem(),) * 4 + (anywhere(),),
        scratch_shapes=[pltpu.VMEM(rolled_probe.shape, jnp.float32)] * 2 + [pltpu.SemaphoreType.DMA],
        cost_estimate=pl.CostEstimate(flops=24 * 2 * 256**3 * 4, bytes_accessed=8 << 20, transcendentals=131072),
        compiler_params=pltpu.CompilerParams(vmem_limit_bytes=16 << 20),
    )(own, core, tile, right_real, right_imag, below_tile, corner_real, corner_imag, rolled_probe, amplitude, tables)


def fold_kernel(parts, copies):
    total = parts[...].sum(0)
    for k in range(copies.shape[0]):
        copies[k] = total


def fold(parts, count):
    return pl.pallas_call(
        fold_kernel,
        out_shape=shape(count, *parts.shape[1:]),
        in_specs=[vmem()],
        out_specs=vmem(),
        cost_estimate=pl.CostEstimate(flops=100000, bytes_accessed=1 << 19, transcendentals=0),
        compiler_params=pltpu.CompilerParams(vmem_limit_bytes=8 << 20),
    )(parts)


def settle_kernel(parts, corner, copies):
    total = parts[...].sum(0)
    new = [corner[part] + total[8 * part : 8 * part + 8] / (total[16:] + 1.0) for part in range(2)]
    both = jnp.concatenate(new, 0)
    for k in range(copies.shape[0]):
        copies[k] = both


def settle(parts, corner, count):
    return pl.pallas_call(
        settle_kernel,
        out_shape=shape(count, 16, SIDE // 2),
        in_specs=[vmem(), vmem()],
        out_specs=vmem(),
        cost_estimate=pl.CostEstimate(flops=100000, bytes_accessed=1 << 19, transcendentals=0),
        compiler_params=pltpu.CompilerParams(vmem_limit_bytes=8 << 20),
    )(parts, corner)


def body(positions, measured, object_field, probe):
    own = positions[0, 0]
    core = lax.axis_index("c")
    corner = lax.dynamic_slice(probe, (0, lax.axis_index(PLANE) * 8, core * (SIDE // 2)), (2, 8, SIDE // 2))
    right_real = passed_along(object_field[0], COL, -1)
    right_imag = passed_along(object_field[1], COL, -1)
    below_tile = passed_along(object_field, ROW, -1)
    rolled_probe = prepare(own, probe)
    right_real, rolled_probe, corner = lax.optimization_barrier((right_real, rolled_probe, corner))
    corner_real = passed_along(right_real, ROW, -1)
    corner_imag = passed_along(right_imag, ROW, -1)
    kept, sent, step_own, step_right, step_row = visit(
        own, core[None], object_field, right_real, right_imag, below_tile, corner_real, corner_imag, rolled_probe,
        measured[0, 0], jnp.asarray(dft_tables()),
    )
    other = lax.ppermute(sent, "c", [(0, 1), (1, 0)])
    rows = SIDE // 8
    pair = (kept + other).reshape(rows, 24, SIDE // 2)
    pair, step_row = lax.optimization_barrier((pair, step_row))
    summed = lax.all_to_all(pair, PLANE, 0, 0)
    step_row = passed_along(step_row, ROW, 1)
    summed = lax.all_to_all(fold(summed, lax.axis_size("y")), "y", 0, 0)
    step_right = passed_along(step_right + step_row[1], COL, 1)
    summed, step_row = lax.optimization_barrier((summed, step_row))
    near = lax.all_to_all(settle(summed, corner, rows), PLANE, 0, 0)
    new_object = finish(own, probe, object_field, step_own, step_row, step_right)
    near, new_object = lax.optimization_barrier((near, new_object))
    far = lax.ppermute(near, "c", [(0, 1), (1, 0)])
    pair = jnp.where(core == 0, jnp.stack([near, far]), jnp.stack([far, near]))
    new_probe = pair.reshape(2, rows, 2, 8, SIDE // 2).transpose(2, 1, 3, 0, 4).reshape(2, SIDE, SIDE)
    return (new_object, new_probe)


def solution(mesh):
    split = Mesh(mesh.devices.reshape(8, 2, 2, 2, 8), ROW + COL)
    in_specs = (P(ROW, COL), P(ROW, COL), P(None, ROW, COL), P())
    out_specs = (P(None, ROW, COL), P())
    return jax.shard_map(body, mesh=split, in_specs=in_specs, out_specs=out_specs, check_vma=False)
```

```python
import math

import jax
import jax.numpy as jnp
import ml_dtypes
import numpy as np
from jax import lax
from jax.experimental import pallas as pl
from jax.experimental.pallas import tpu as pltpu
from jax.sharding import Mesh
from jax.sharding import PartitionSpec as P

SIDE = 256
ROW = ("y", "xh", "c")
COL = ("xl", "z")
PLANE = ("xh", "xl", "z")


def passed_along(value, axis, steps):
    count = lax.axis_size(axis)
    leading, last = (max(0, -steps), min(count, count - steps))
    return lax.ppermute(value, axis, [(source, source + steps) for source in range(leading, last)])


def dft_tables():
    indices = np.arange(SIDE)
    angles = (indices[:, None] * indices[None, :] % SIDE) * (2.0 * math.pi / SIDE)
    cosine, sine = np.cos(angles) / math.sqrt(SIDE), np.sin(angles) / math.sqrt(SIDE)
    three = np.stack([cosine, sine, -sine])
    head = three.astype(ml_dtypes.bfloat16)
    rest = (three - head.astype(np.float64)).astype(ml_dtypes.bfloat16)
    return np.stack([head, rest], 1)


def halves(value):
    head = value.astype(jnp.bfloat16)
    return head, (value - head.astype(jnp.float32)).astype(jnp.bfloat16)


def dot(left, right):
    return jnp.dot(left, right, preferred_element_type=jnp.float32)


def block(tables, sign, which):
    up, down = (1, 2) if sign > 0 else (2, 1)
    upper = jnp.concatenate([tables[0, which], tables[up, which]], 1)
    return jnp.concatenate([upper, jnp.concatenate([tables[down, which], tables[0, which]], 1)], 0)


def apply_left(tables, sign, value):
    head, rest = halves(value)
    matrix = block(tables, sign, 0)
    return dot(matrix, head) + dot(matrix, rest) + dot(block(tables, sign, 1), head)


def apply_right(tables, sign, value):
    head, rest = halves(value)
    matrix = block(tables, sign, 0)
    return dot(head, matrix) + dot(rest, matrix) + dot(head, block(tables, sign, 1))


def to_columns(value):
    return jnp.concatenate(
        [jnp.concatenate([value[:SIDE, k * SIDE : (k + 1) * SIDE], value[SIDE:, k * SIDE : (k + 1) * SIDE]], 1) for k in range(2)], 0
    )


def rolled(value, rows, cols):
    return pltpu.roll(pltpu.roll(value, rows, 0), cols, 1)


def quadrants(row, col):
    below = lax.broadcasted_iota(jnp.int32, (SIDE, SIDE), 0) < row
    right = lax.broadcasted_iota(jnp.int32, (SIDE, SIDE), 1) < col
    return below, right


def prepare_kernel(own, probe, rolled_probe):
    for k in range(2):
        for part in range(2):
            rolled_probe[k, part] = rolled(probe[part], own[k, 0], own[k, 1])


def carried(block, first):
    line = lax.broadcasted_iota(jnp.int32, block.shape, 0)
    last = lax.broadcasted_iota(jnp.int32, block.shape, 1) == block.shape[1] - 1
    return [jnp.sum(jnp.where(last & (line == first + k), block, 0.0)).astype(jnp.int32) for k in range(4)]


def finish_kernel(own, probe, tile, step_own, step_row, step_right, new_tile):
    half = SIDE // 2
    intensity = probe[0] * probe[0] + probe[1] * probe[1]
    beside, above = step_right[0, :8, half:], step_row[1, 0, :8, half:]
    total = jnp.ones((SIDE, SIDE), jnp.float32)
    for spots, lies_below, lies_right in (
        ([own[k // 2, k % 2] for k in range(4)], False, False),
        (carried(beside, 4), False, True),
        (carried(above, 0), True, False),
        (carried(beside, 0), True, True),
    ):
        for k in range(2):
            row, col = spots[2 * k], spots[2 * k + 1]
            below, right = quadrants(row, col)
            inside = (below == lies_below) & (right == lies_right)
            total += jnp.where(inside, rolled(intensity, row, col), 0.0)
    last = lax.broadcasted_iota(jnp.int32, (SIDE, SIDE), 1) == SIDE - 1
    for part in range(2):
        arrived = step_row[0, part] + jnp.where(last, 0.0, step_right[part])
        new_tile[part] = tile[part] + (step_own[part] + arrived) / total


def visit_kernel(
    own, core, tile, right_real, right_imag, below_tile, corner_real, corner_imag, rolled_probe, amplitude,
    tables, kept, sent, step_own, step_right, step_row, patches, near_row, stored,
):
    right_tile, corner_tile = (right_real, right_imag), (corner_real, corner_imag)
    exits = []
    for k in range(2):
        below, right = quadrants(own[k, 0], own[k, 1])
        for part in range(2):
            patches[k, part] = jnp.where(
                below,
                jnp.where(right, corner_tile[part][...], below_tile[part]),
                jnp.where(right, right_tile[part][...], tile[part]),
            )
        pr, pi = rolled_probe[k, 0], rolled_probe[k, 1]
        qr, qi = patches[k, 0], patches[k, 1]
        exits.append(jnp.concatenate([pr * qr - pi * qi, pr * qi + pi * qr], 0))
    exits = jnp.concatenate(exits, 1)
    field = to_columns(apply_left(tables, 1, exits))
    far = apply_right(tables, -1, field)
    far_real, far_imag = far[:, :SIDE], far[:, SIDE:]
    power = jnp.maximum(far_real * far_real + far_imag * far_imag, 0.25)
    factor = amplitude[...].reshape(2 * SIDE, SIDE).astype(jnp.float32) * lax.rsqrt(power) - 1.0
    change_real, change_imag = far_real * factor, far_imag * factor
    change = jnp.concatenate(
        [jnp.concatenate([change_real[k * SIDE : (k + 1) * SIDE], change_imag[k * SIDE : (k + 1) * SIDE]], 0) for k in range(2)], 1
    )
    chi = apply_right(tables, 1, to_columns(apply_left(tables, -1, change)))
    numerator = [jnp.zeros((SIDE, SIDE), jnp.float32)] * 3
    for k in range(2):
        chi_real = chi[k * SIDE : (k + 1) * SIDE, :SIDE]
        chi_imag = chi[k * SIDE : (k + 1) * SIDE, SIDE:]
        qr, qi = patches[k, 0], patches[k, 1]
        back_row, back_col = (SIDE - own[k, 0]) & (SIDE - 1), (SIDE - own[k, 1]) & (SIDE - 1)
        terms = (qr * chi_real + qi * chi_imag, qr * chi_imag - qi * chi_real, qr * qr + qi * qi)
        numerator = [total + rolled(term, back_row, back_col) for total, term in zip(numerator, terms)]
    first = core[0] == 0
    half = SIDE // 2
    for layer in range(3):
        one, other = numerator[layer][:, :half], numerator[layer][:, half:]
        kept[:, layer] = jnp.where(first, one, other).reshape(SIDE // 8, 8, half)
        sent[:, layer] = jnp.where(first, other, one).reshape(SIDE // 8, 8, half)
    line = lax.broadcasted_iota(jnp.int32, (8, half), 0)
    last = lax.broadcasted_iota(jnp.int32, (8, half), 1) == half - 1
    spots = jnp.zeros((8, half), jnp.int32)
    for k in range(4):
        spots = jnp.where((line & 3) == k, own[k // 2, k % 2], spots)
    spots = spots.astype(jnp.float32)

    def step(part, inside):
        total = jnp.zeros((SIDE, SIDE), jnp.float32)
        for k in range(2):
            chi_real = chi[k * SIDE : (k + 1) * SIDE, :SIDE]
            chi_imag = chi[k * SIDE : (k + 1) * SIDE, SIDE:]
            pr, pi = rolled_probe[k, 0], rolled_probe[k, 1]
            term = pr * chi_imag - pi * chi_real if part else pr * chi_real + pi * chi_imag
            total += jnp.where(inside(*quadrants(own[k, 0], own[k, 1])), term, 0.0)
        return total

    for part in range(2):
        near_row[0, part] = step(part, lambda below, right: below & jnp.logical_not(right))
        near_row[1, part] = step(part, lambda below, right: below & right)
    near_row[1, 0, :8, half:] = jnp.where(last & (line < 4), spots, near_row[1, 0, :8, half:])
    store = pltpu.make_async_copy(near_row, step_row, stored)
    store.start()
    for part in range(2):
        step_right[part] = step(part, lambda below, right: right & jnp.logical_not(below))
        step_own[part] = step(part, lambda below, right: jnp.logical_not(below | right))
    step_right[0, :8, half:] = jnp.where(last & (line >= 4), spots, step_right[0, :8, half:])
    store.wait()


def vmem():
    return pl.BlockSpec(memory_space=pltpu.VMEM)


def smem():
    return pl.BlockSpec(memory_space=pltpu.SMEM)


def shape(*sizes):
    return jax.ShapeDtypeStruct(sizes, jnp.float32)


def anywhere():
    return pl.BlockSpec(memory_space=pl.ANY)


def prepare(own, probe):
    return pl.pallas_call(
        prepare_kernel,
        out_shape=shape(2, 2, SIDE, SIDE),
        in_specs=[smem(), vmem()],
        out_specs=vmem(),
        cost_estimate=pl.CostEstimate(flops=2000000, bytes_accessed=2 << 20, transcendentals=0),
        compiler_params=pltpu.CompilerParams(vmem_limit_bytes=16 << 20),
    )(own, probe)


def finish(own, probe, tile, step_own, step_row, step_right):
    return pl.pallas_call(
        finish_kernel,
        out_shape=shape(2, SIDE, SIDE),
        in_specs=[smem()] + [vmem()] * 5,
        out_specs=vmem(),
        cost_estimate=pl.CostEstimate(flops=8000000, bytes_accessed=8 << 20, transcendentals=0),
        compiler_params=pltpu.CompilerParams(vmem_limit_bytes=16 << 20),
    )(own, probe, tile, step_own, step_row, step_right)


def visit(own, core, tile, right_real, right_imag, below_tile, corner_real, corner_imag, rolled_probe, amplitude, tables):
    rows = SIDE // 8
    out_shape = (
        shape(rows, 3, 8, SIDE // 2),
        shape(rows, 3, 8, SIDE // 2),
        shape(2, SIDE, SIDE),
        shape(2, SIDE, SIDE),
        shape(2, 2, SIDE, SIDE),
    )
    return pl.pallas_call(
        visit_kernel,
        out_shape=out_shape,
        in_specs=[smem(), smem()] + [vmem()] * 9,
        out_specs=(vmem(),) * 4 + (anywhere(),),
        scratch_shapes=[pltpu.VMEM(rolled_probe.shape, jnp.float32)] * 2 + [pltpu.SemaphoreType.DMA],
        cost_estimate=pl.CostEstimate(flops=24 * 2 * 256**3 * 4, bytes_accessed=8 << 20, transcendentals=131072),
        compiler_params=pltpu.CompilerParams(vmem_limit_bytes=16 << 20),
    )(own, core, tile, right_real, right_imag, below_tile, corner_real, corner_imag, rolled_probe, amplitude, tables)


def fold_kernel(parts, copies):
    total = parts[...].sum(0)
    for k in range(copies.shape[0]):
        copies[k] = total


def fold(parts, count):
    return pl.pallas_call(
        fold_kernel,
        out_shape=shape(count, *parts.shape[1:]),
        in_specs=[vmem()],
        out_specs=vmem(),
        cost_estimate=pl.CostEstimate(flops=4000000000, bytes_accessed=1 << 19, transcendentals=0),
        compiler_params=pltpu.CompilerParams(vmem_limit_bytes=8 << 20),
    )(parts)


def settle_kernel(parts, corner, copies):
    total = parts[...].sum(0)
    new = [corner[part] + total[8 * part : 8 * part + 8] / (total[16:] + 1.0) for part in range(2)]
    both = jnp.concatenate(new, 0)
    for k in range(copies.shape[0]):
        copies[k] = both


def settle(parts, corner, count):
    return pl.pallas_call(
        settle_kernel,
        out_shape=shape(count, 16, SIDE // 2),
        in_specs=[vmem(), vmem()],
        out_specs=vmem(),
        cost_estimate=pl.CostEstimate(flops=100000, bytes_accessed=1 << 19, transcendentals=0),
        compiler_params=pltpu.CompilerParams(vmem_limit_bytes=8 << 20),
    )(parts, corner)


def body(positions, measured, object_field, probe):
    own = positions[0, 0]
    core = lax.axis_index("c")
    corner = lax.dynamic_slice(probe, (0, lax.axis_index(PLANE) * 8, core * (SIDE // 2)), (2, 8, SIDE // 2))
    right_real = passed_along(object_field[0], COL, -1)
    right_imag = passed_along(object_field[1], COL, -1)
    below_tile = passed_along(object_field, ROW, -1)
    rolled_probe = prepare(own, probe)
    right_real, rolled_probe, corner = lax.optimization_barrier((right_real, rolled_probe, corner))
    corner_real = passed_along(right_real, ROW, -1)
    corner_imag = passed_along(right_imag, ROW, -1)
    kept, sent, step_own, step_right, step_row = visit(
        own, core[None], object_field, right_real, right_imag, below_tile, corner_real, corner_imag, rolled_probe,
        measured[0, 0], jnp.asarray(dft_tables()),
    )
    other = lax.ppermute(sent, "c", [(0, 1), (1, 0)])
    rows = SIDE // 8
    pair = (kept + other).reshape(rows, 24, SIDE // 2)
    pair, step_row = lax.optimization_barrier((pair, step_row))
    summed = lax.all_to_all(pair, PLANE, 0, 0)
    step_row = passed_along(step_row, ROW, 1)
    summed = lax.all_to_all(fold(summed, lax.axis_size("y")), "y", 0, 0)
    step_right = passed_along(step_right + step_row[1], COL, 1)
    summed, step_row = lax.optimization_barrier((summed, step_row))
    near = lax.all_to_all(settle(summed, corner, rows), PLANE, 0, 0)
    new_object = finish(own, probe, object_field, step_own, step_row, step_right)
    near, new_object = lax.optimization_barrier((near, new_object))
    far = lax.ppermute(near, "c", [(0, 1), (1, 0)])
    pair = jnp.where(core == 0, jnp.stack([near, far]), jnp.stack([far, near]))
    new_probe = pair.reshape(2, rows, 2, 8, SIDE // 2).transpose(2, 1, 3, 0, 4).reshape(2, SIDE, SIDE)
    return (new_object, new_probe)


def solution(mesh):
    split = Mesh(mesh.devices.reshape(8, 2, 2, 2, 8), ROW + COL)
    in_specs = (P(ROW, COL), P(ROW, COL), P(None, ROW, COL), P())
    out_specs = (P(None, ROW, COL), P())
    return jax.shard_map(body, mesh=split, in_specs=in_specs, out_specs=out_specs, check_vma=False)
```

```python
import math

import jax
import jax.numpy as jnp
import ml_dtypes
import numpy as np
from jax import lax
from jax.experimental import pallas as pl
from jax.experimental.pallas import tpu as pltpu
from jax.sharding import Mesh
from jax.sharding import PartitionSpec as P

SIDE = 256
ROW = ("y", "xh", "c")
COL = ("xl", "z")
PLANE = ("xh", "xl", "z")


def passed_along(value, axis, steps):
    count = lax.axis_size(axis)
    leading, last = (max(0, -steps), min(count, count - steps))
    return lax.ppermute(value, axis, [(source, source + steps) for source in range(leading, last)])


def dft_tables():
    indices = np.arange(SIDE)
    angles = (indices[:, None] * indices[None, :] % SIDE) * (2.0 * math.pi / SIDE)
    cosine, sine = np.cos(angles) / math.sqrt(SIDE), np.sin(angles) / math.sqrt(SIDE)
    three = np.stack([cosine, sine, -sine])
    head = three.astype(ml_dtypes.bfloat16)
    rest = (three - head.astype(np.float64)).astype(ml_dtypes.bfloat16)
    return np.stack([head, rest], 1)


def halves(value):
    head = value.astype(jnp.bfloat16)
    return head, (value - head.astype(jnp.float32)).astype(jnp.bfloat16)


def dot(left, right):
    return jnp.dot(left, right, preferred_element_type=jnp.float32)


def block(tables, sign, which):
    up, down = (1, 2) if sign > 0 else (2, 1)
    upper = jnp.concatenate([tables[0, which], tables[up, which]], 1)
    return jnp.concatenate([upper, jnp.concatenate([tables[down, which], tables[0, which]], 1)], 0)


def apply_left(tables, sign, value):
    head, rest = halves(value)
    matrix = block(tables, sign, 0)
    return dot(matrix, head) + dot(matrix, rest) + dot(block(tables, sign, 1), head)


def apply_right(tables, sign, value):
    head, rest = halves(value)
    matrix = block(tables, sign, 0)
    return dot(head, matrix) + dot(rest, matrix) + dot(head, block(tables, sign, 1))


def to_columns(value):
    return jnp.concatenate(
        [jnp.concatenate([value[:SIDE, k * SIDE : (k + 1) * SIDE], value[SIDE:, k * SIDE : (k + 1) * SIDE]], 1) for k in range(2)], 0
    )


def rolled(value, rows, cols):
    return pltpu.roll(pltpu.roll(value, rows, 0), cols, 1)


def quadrants(row, col):
    below = lax.broadcasted_iota(jnp.int32, (SIDE, SIDE), 0) < row
    right = lax.broadcasted_iota(jnp.int32, (SIDE, SIDE), 1) < col
    return below, right


def prepare_kernel(own, probe, rolled_probe):
    for k in range(2):
        for part in range(2):
            rolled_probe[k, part] = rolled(probe[part], own[k, 0], own[k, 1])


def carried(block, first):
    line = lax.broadcasted_iota(jnp.int32, block.shape, 0)
    last = lax.broadcasted_iota(jnp.int32, block.shape, 1) == block.shape[1] - 1
    return [jnp.sum(jnp.where(last & (line == first + k), block, 0.0)).astype(jnp.int32) for k in range(4)]


def finish_kernel(own, probe, tile, step_own, step_row, step_right, new_tile):
    half = SIDE // 2
    intensity = probe[0] * probe[0] + probe[1] * probe[1]
    beside, above = step_right[0, :8, half:], step_row[1, 0, :8, half:]
    total = jnp.ones((SIDE, SIDE), jnp.float32)
    for spots, lies_below, lies_right in (
        ([own[k // 2, k % 2] for k in range(4)], False, False),
        (carried(beside, 4), False, True),
        (carried(above, 0), True, False),
        (carried(beside, 0), True, True),
    ):
        for k in range(2):
            row, col = spots[2 * k], spots[2 * k + 1]
            below, right = quadrants(row, col)
            inside = (below == lies_below) & (right == lies_right)
            total += jnp.where(inside, rolled(intensity, row, col), 0.0)
    last = lax.broadcasted_iota(jnp.int32, (SIDE, SIDE), 1) == SIDE - 1
    for part in range(2):
        arrived = step_row[0, part] + jnp.where(last, 0.0, step_right[part])
        new_tile[part] = tile[part] + (step_own[part] + arrived) / total


def visit_kernel(
    own, core, tile, right_real, right_imag, below_tile, corner_real, corner_imag, rolled_probe, amplitude,
    tables, kept, sent, step_own, step_right, step_row, patches,
):
    right_tile, corner_tile = (right_real, right_imag), (corner_real, corner_imag)
    exits = []
    for k in range(2):
        below, right = quadrants(own[k, 0], own[k, 1])
        for part in range(2):
            patches[k, part] = jnp.where(
                below,
                jnp.where(right, corner_tile[part][...], below_tile[part]),
                jnp.where(right, right_tile[part][...], tile[part]),
            )
        pr, pi = rolled_probe[k, 0], rolled_probe[k, 1]
        qr, qi = patches[k, 0], patches[k, 1]
        exits.append(jnp.concatenate([pr * qr - pi * qi, pr * qi + pi * qr], 0))
    exits = jnp.concatenate(exits, 1)
    field = to_columns(apply_left(tables, 1, exits))
    far = apply_right(tables, -1, field)
    far_real, far_imag = far[:, :SIDE], far[:, SIDE:]
    power = jnp.maximum(far_real * far_real + far_imag * far_imag, 0.25)
    factor = amplitude[...].reshape(2 * SIDE, SIDE).astype(jnp.float32) * lax.rsqrt(power) - 1.0
    change_real, change_imag = far_real * factor, far_imag * factor
    change = jnp.concatenate(
        [jnp.concatenate([change_real[k * SIDE : (k + 1) * SIDE], change_imag[k * SIDE : (k + 1) * SIDE]], 0) for k in range(2)], 1
    )
    chi = apply_right(tables, 1, to_columns(apply_left(tables, -1, change)))
    numerator = [jnp.zeros((SIDE, SIDE), jnp.float32)] * 3
    for k in range(2):
        chi_real = chi[k * SIDE : (k + 1) * SIDE, :SIDE]
        chi_imag = chi[k * SIDE : (k + 1) * SIDE, SIDE:]
        qr, qi = patches[k, 0], patches[k, 1]
        back_row, back_col = (SIDE - own[k, 0]) & (SIDE - 1), (SIDE - own[k, 1]) & (SIDE - 1)
        terms = (qr * chi_real + qi * chi_imag, qr * chi_imag - qi * chi_real, qr * qr + qi * qi)
        numerator = [total + rolled(term, back_row, back_col) for total, term in zip(numerator, terms)]
    first = core[0] == 0
    half = SIDE // 2
    for layer in range(3):
        one, other = numerator[layer][:, :half], numerator[layer][:, half:]
        kept[:, layer] = jnp.where(first, one, other).reshape(SIDE // 8, 8, half)
        sent[:, layer] = jnp.where(first, other, one).reshape(SIDE // 8, 8, half)
    line = lax.broadcasted_iota(jnp.int32, (8, half), 0)
    last = lax.broadcasted_iota(jnp.int32, (8, half), 1) == half - 1
    spots = jnp.zeros((8, half), jnp.int32)
    for k in range(4):
        spots = jnp.where((line & 3) == k, own[k // 2, k % 2], spots)
    spots = spots.astype(jnp.float32)

    def step(part, inside):
        total = jnp.zeros((SIDE, SIDE), jnp.float32)
        for k in range(2):
            chi_real = chi[k * SIDE : (k + 1) * SIDE, :SIDE]
            chi_imag = chi[k * SIDE : (k + 1) * SIDE, SIDE:]
            pr, pi = rolled_probe[k, 0], rolled_probe[k, 1]
            term = pr * chi_imag - pi * chi_real if part else pr * chi_real + pi * chi_imag
            total += jnp.where(inside(*quadrants(own[k, 0], own[k, 1])), term, 0.0)
        return total

    for part in range(2):
        step_row[0, part] = step(part, lambda below, right: below & jnp.logical_not(right))
        step_row[1, part] = step(part, lambda below, right: below & right)
    step_row[1, 0, :8, half:] = jnp.where(last & (line < 4), spots, step_row[1, 0, :8, half:])
    for part in range(2):
        step_right[part] = step(part, lambda below, right: right & jnp.logical_not(below))
        step_own[part] = step(part, lambda below, right: jnp.logical_not(below | right))
    step_right[0, :8, half:] = jnp.where(last & (line >= 4), spots, step_right[0, :8, half:])


def vmem():
    return pl.BlockSpec(memory_space=pltpu.VMEM)


def smem():
    return pl.BlockSpec(memory_space=pltpu.SMEM)


def shape(*sizes):
    return jax.ShapeDtypeStruct(sizes, jnp.float32)


def anywhere():
    return pl.BlockSpec(memory_space=pl.ANY)


def prepare(own, probe):
    return pl.pallas_call(
        prepare_kernel,
        out_shape=shape(2, 2, SIDE, SIDE),
        in_specs=[smem(), vmem()],
        out_specs=vmem(),
        cost_estimate=pl.CostEstimate(flops=2000000, bytes_accessed=2 << 20, transcendentals=0),
        compiler_params=pltpu.CompilerParams(vmem_limit_bytes=16 << 20),
    )(own, probe)


def finish(own, probe, tile, step_own, step_row, step_right):
    return pl.pallas_call(
        finish_kernel,
        out_shape=shape(2, SIDE, SIDE),
        in_specs=[smem()] + [vmem()] * 5,
        out_specs=vmem(),
        cost_estimate=pl.CostEstimate(flops=8000000, bytes_accessed=8 << 20, transcendentals=0),
        compiler_params=pltpu.CompilerParams(vmem_limit_bytes=16 << 20),
    )(own, probe, tile, step_own, step_row, step_right)


def visit(own, core, tile, right_real, right_imag, below_tile, corner_real, corner_imag, rolled_probe, amplitude, tables):
    rows = SIDE // 8
    out_shape = (
        shape(rows, 3, 8, SIDE // 2),
        shape(rows, 3, 8, SIDE // 2),
        shape(2, SIDE, SIDE),
        shape(2, SIDE, SIDE),
        shape(2, 2, SIDE, SIDE),
    )
    return pl.pallas_call(
        visit_kernel,
        out_shape=out_shape,
        in_specs=[smem(), smem()] + [vmem()] * 9,
        out_specs=(vmem(),) * 5,
        scratch_shapes=[pltpu.VMEM(rolled_probe.shape, jnp.float32)],
        cost_estimate=pl.CostEstimate(flops=24 * 2 * 256**3 * 4, bytes_accessed=8 << 20, transcendentals=131072),
        compiler_params=pltpu.CompilerParams(vmem_limit_bytes=16 << 20),
    )(own, core, tile, right_real, right_imag, below_tile, corner_real, corner_imag, rolled_probe, amplitude, tables)


def fold_kernel(parts, copies):
    total = parts[...].sum(0)
    for k in range(copies.shape[0]):
        copies[k] = total


def fold(parts, count):
    return pl.pallas_call(
        fold_kernel,
        out_shape=shape(count, *parts.shape[1:]),
        in_specs=[vmem()],
        out_specs=vmem(),
        cost_estimate=pl.CostEstimate(flops=4000000000, bytes_accessed=1 << 19, transcendentals=0),
        compiler_params=pltpu.CompilerParams(vmem_limit_bytes=8 << 20),
    )(parts)


def settle_kernel(parts, corner, copies):
    total = parts[...].sum(0)
    new = [corner[part] + total[8 * part : 8 * part + 8] / (total[16:] + 1.0) for part in range(2)]
    both = jnp.concatenate(new, 0)
    for k in range(copies.shape[0]):
        copies[k] = both


def settle(parts, corner, count):
    return pl.pallas_call(
        settle_kernel,
        out_shape=shape(count, 16, SIDE // 2),
        in_specs=[vmem(), vmem()],
        out_specs=vmem(),
        cost_estimate=pl.CostEstimate(flops=100000, bytes_accessed=1 << 19, transcendentals=0),
        compiler_params=pltpu.CompilerParams(vmem_limit_bytes=8 << 20),
    )(parts, corner)


def body(positions, measured, object_field, probe):
    own = positions[0, 0]
    core = lax.axis_index("c")
    corner = lax.dynamic_slice(probe, (0, lax.axis_index(PLANE) * 8, core * (SIDE // 2)), (2, 8, SIDE // 2))
    right_real = passed_along(object_field[0], COL, -1)
    right_imag = passed_along(object_field[1], COL, -1)
    below_tile = passed_along(object_field, ROW, -1)
    rolled_probe = prepare(own, probe)
    right_real, rolled_probe, corner = lax.optimization_barrier((right_real, rolled_probe, corner))
    corner_real = passed_along(right_real, ROW, -1)
    corner_imag = passed_along(right_imag, ROW, -1)
    kept, sent, step_own, step_right, step_row = visit(
        own, core[None], object_field, right_real, right_imag, below_tile, corner_real, corner_imag, rolled_probe,
        measured[0, 0], jnp.asarray(dft_tables()),
    )
    other = lax.ppermute(sent, "c", [(0, 1), (1, 0)])
    rows = SIDE // 8
    pair = (kept + other).reshape(rows, 24, SIDE // 2)
    pair, step_row = lax.optimization_barrier((pair, step_row))
    summed = lax.all_to_all(pair, PLANE, 0, 0)
    step_row = passed_along(step_row, ROW, 1)
    summed = lax.all_to_all(fold(summed, lax.axis_size("y")), "y", 0, 0)
    step_right = passed_along(step_right + step_row[1], COL, 1)
    summed, step_row = lax.optimization_barrier((summed, step_row))
    near = lax.all_to_all(settle(summed, corner, rows), PLANE, 0, 0)
    new_object = finish(own, probe, object_field, step_own, step_row, step_right)
    near, new_object = lax.optimization_barrier((near, new_object))
    far = lax.ppermute(near, "c", [(0, 1), (1, 0)])
    pair = jnp.where(core == 0, jnp.stack([near, far]), jnp.stack([far, near]))
    new_probe = pair.reshape(2, rows, 2, 8, SIDE // 2).transpose(2, 1, 3, 0, 4).reshape(2, SIDE, SIDE)
    return (new_object, new_probe)


def solution(mesh):
    split = Mesh(mesh.devices.reshape(8, 2, 2, 2, 8), ROW + COL)
    in_specs = (P(ROW, COL), P(ROW, COL), P(None, ROW, COL), P())
    out_specs = (P(None, ROW, COL), P())
    return jax.shard_map(body, mesh=split, in_specs=in_specs, out_specs=out_specs, check_vma=False)
```

```python
import math

import jax
import jax.numpy as jnp
import ml_dtypes
import numpy as np
from jax import lax
from jax.experimental import pallas as pl
from jax.experimental.pallas import tpu as pltpu
from jax.sharding import Mesh
from jax.sharding import PartitionSpec as P

SIDE = 256
ROW = ("y", "xh", "c")
COL = ("xl", "z")
PLANE = ("xl", "xh", "z")


def passed_along(value, axis, steps):
    count = lax.axis_size(axis)
    leading, last = (max(0, -steps), min(count, count - steps))
    return lax.ppermute(value, axis, [(source, source + steps) for source in range(leading, last)])


def dft_tables():
    indices = np.arange(SIDE)
    angles = (indices[:, None] * indices[None, :] % SIDE) * (2.0 * math.pi / SIDE)
    cosine, sine = np.cos(angles) / math.sqrt(SIDE), np.sin(angles) / math.sqrt(SIDE)
    three = np.stack([cosine, sine, -sine])
    head = three.astype(ml_dtypes.bfloat16)
    rest = (three - head.astype(np.float64)).astype(ml_dtypes.bfloat16)
    return np.stack([head, rest], 1)


def halves(value):
    head = value.astype(jnp.bfloat16)
    return head, (value - head.astype(jnp.float32)).astype(jnp.bfloat16)


def dot(left, right):
    return jnp.dot(left, right, preferred_element_type=jnp.float32)


def block(tables, sign, which):
    up, down = (1, 2) if sign > 0 else (2, 1)
    upper = jnp.concatenate([tables[0, which], tables[up, which]], 1)
    return jnp.concatenate([upper, jnp.concatenate([tables[down, which], tables[0, which]], 1)], 0)


def apply_left(tables, sign, value):
    head, rest = halves(value)
    matrix = block(tables, sign, 0)
    return dot(matrix, head) + dot(matrix, rest) + dot(block(tables, sign, 1), head)


def apply_right(tables, sign, value):
    head, rest = halves(value)
    matrix = block(tables, sign, 0)
    return dot(head, matrix) + dot(rest, matrix) + dot(head, block(tables, sign, 1))


def to_columns(value):
    return jnp.concatenate(
        [jnp.concatenate([value[:SIDE, k * SIDE : (k + 1) * SIDE], value[SIDE:, k * SIDE : (k + 1) * SIDE]], 1) for k in range(2)], 0
    )


def rolled(value, rows, cols):
    return pltpu.roll(pltpu.roll(value, rows, 0), cols, 1)


def quadrants(row, col):
    below = lax.broadcasted_iota(jnp.int32, (SIDE, SIDE), 0) < row
    right = lax.broadcasted_iota(jnp.int32, (SIDE, SIDE), 1) < col
    return below, right


def prepare_kernel(own, probe, rolled_probe):
    for k in range(2):
        for part in range(2):
            rolled_probe[k, part] = rolled(probe[part], own[k, 0], own[k, 1])


def carried(block, first):
    line = lax.broadcasted_iota(jnp.int32, block.shape, 0)
    last = lax.broadcasted_iota(jnp.int32, block.shape, 1) == block.shape[1] - 1
    return [jnp.sum(jnp.where(last & (line == first + k), block, 0.0)).astype(jnp.int32) for k in range(4)]


def finish_kernel(own, probe, tile, step_own, step_row, step_right, new_tile):
    half = SIDE // 2
    intensity = probe[0] * probe[0] + probe[1] * probe[1]
    beside, above = step_right[0, :8, half:], step_row[1, 0, :8, half:]
    total = jnp.ones((SIDE, SIDE), jnp.float32)
    for spots, lies_below, lies_right in (
        ([own[k // 2, k % 2] for k in range(4)], False, False),
        (carried(beside, 4), False, True),
        (carried(above, 0), True, False),
        (carried(beside, 0), True, True),
    ):
        for k in range(2):
            row, col = spots[2 * k], spots[2 * k + 1]
            below, right = quadrants(row, col)
            inside = (below == lies_below) & (right == lies_right)
            total += jnp.where(inside, rolled(intensity, row, col), 0.0)
    last = lax.broadcasted_iota(jnp.int32, (SIDE, SIDE), 1) == SIDE - 1
    for part in range(2):
        arrived = step_row[0, part] + jnp.where(last, 0.0, step_right[part])
        new_tile[part] = tile[part] + (step_own[part] + arrived) / total


def visit_kernel(
    own, core, tile, right_real, right_imag, below_tile, corner_real, corner_imag, rolled_probe, amplitude,
    tables, kept, sent, step_own, step_right, step_row, patches,
):
    right_tile, corner_tile = (right_real, right_imag), (corner_real, corner_imag)
    exits = []
    for k in range(2):
        below, right = quadrants(own[k, 0], own[k, 1])
        for part in range(2):
            patches[k, part] = jnp.where(
                below,
                jnp.where(right, corner_tile[part][...], below_tile[part]),
                jnp.where(right, right_tile[part][...], tile[part]),
            )
        pr, pi = rolled_probe[k, 0], rolled_probe[k, 1]
        qr, qi = patches[k, 0], patches[k, 1]
        exits.append(jnp.concatenate([pr * qr - pi * qi, pr * qi + pi * qr], 0))
    exits = jnp.concatenate(exits, 1)
    field = to_columns(apply_left(tables, 1, exits))
    far = apply_right(tables, -1, field)
    far_real, far_imag = far[:, :SIDE], far[:, SIDE:]
    power = jnp.maximum(far_real * far_real + far_imag * far_imag, 0.25)
    factor = amplitude[...].reshape(2 * SIDE, SIDE).astype(jnp.float32) * lax.rsqrt(power) - 1.0
    change_real, change_imag = far_real * factor, far_imag * factor
    change = jnp.concatenate(
        [jnp.concatenate([change_real[k * SIDE : (k + 1) * SIDE], change_imag[k * SIDE : (k + 1) * SIDE]], 0) for k in range(2)], 1
    )
    chi = apply_right(tables, 1, to_columns(apply_left(tables, -1, change)))
    numerator = [jnp.zeros((SIDE, SIDE), jnp.float32)] * 3
    for k in range(2):
        chi_real = chi[k * SIDE : (k + 1) * SIDE, :SIDE]
        chi_imag = chi[k * SIDE : (k + 1) * SIDE, SIDE:]
        qr, qi = patches[k, 0], patches[k, 1]
        back_row, back_col = (SIDE - own[k, 0]) & (SIDE - 1), (SIDE - own[k, 1]) & (SIDE - 1)
        terms = (qr * chi_real + qi * chi_imag, qr * chi_imag - qi * chi_real, qr * qr + qi * qi)
        numerator = [total + rolled(term, back_row, back_col) for total, term in zip(numerator, terms)]
    first = core[0] == 0
    half = SIDE // 2
    for layer in range(3):
        one, other = numerator[layer][:, :half], numerator[layer][:, half:]
        kept[:, layer] = jnp.where(first, one, other).reshape(SIDE // 8, 8, half)
        sent[:, layer] = jnp.where(first, other, one).reshape(SIDE // 8, 8, half)
    line = lax.broadcasted_iota(jnp.int32, (8, half), 0)
    last = lax.broadcasted_iota(jnp.int32, (8, half), 1) == half - 1
    spots = jnp.zeros((8, half), jnp.int32)
    for k in range(4):
        spots = jnp.where((line & 3) == k, own[k // 2, k % 2], spots)
    spots = spots.astype(jnp.float32)

    def step(part, inside):
        total = jnp.zeros((SIDE, SIDE), jnp.float32)
        for k in range(2):
            chi_real = chi[k * SIDE : (k + 1) * SIDE, :SIDE]
            chi_imag = chi[k * SIDE : (k + 1) * SIDE, SIDE:]
            pr, pi = rolled_probe[k, 0], rolled_probe[k, 1]
            term = pr * chi_imag - pi * chi_real if part else pr * chi_real + pi * chi_imag
            total += jnp.where(inside(*quadrants(own[k, 0], own[k, 1])), term, 0.0)
        return total

    for part in range(2):
        step_row[0, part] = step(part, lambda below, right: below & jnp.logical_not(right))
        step_row[1, part] = step(part, lambda below, right: below & right)
    step_row[1, 0, :8, half:] = jnp.where(last & (line < 4), spots, step_row[1, 0, :8, half:])
    for part in range(2):
        step_right[part] = step(part, lambda below, right: right & jnp.logical_not(below))
        step_own[part] = step(part, lambda below, right: jnp.logical_not(below | right))
    step_right[0, :8, half:] = jnp.where(last & (line >= 4), spots, step_right[0, :8, half:])


def vmem():
    return pl.BlockSpec(memory_space=pltpu.VMEM)


def smem():
    return pl.BlockSpec(memory_space=pltpu.SMEM)


def shape(*sizes):
    return jax.ShapeDtypeStruct(sizes, jnp.float32)


def anywhere():
    return pl.BlockSpec(memory_space=pl.ANY)


def prepare(own, probe):
    return pl.pallas_call(
        prepare_kernel,
        out_shape=shape(2, 2, SIDE, SIDE),
        in_specs=[smem(), vmem()],
        out_specs=vmem(),
        cost_estimate=pl.CostEstimate(flops=2000000, bytes_accessed=2 << 20, transcendentals=0),
        compiler_params=pltpu.CompilerParams(vmem_limit_bytes=16 << 20),
    )(own, probe)


def finish(own, probe, tile, step_own, step_row, step_right):
    return pl.pallas_call(
        finish_kernel,
        out_shape=shape(2, SIDE, SIDE),
        in_specs=[smem()] + [vmem()] * 5,
        out_specs=vmem(),
        cost_estimate=pl.CostEstimate(flops=8000000, bytes_accessed=8 << 20, transcendentals=0),
        compiler_params=pltpu.CompilerParams(vmem_limit_bytes=16 << 20),
    )(own, probe, tile, step_own, step_row, step_right)


def visit(own, core, tile, right_real, right_imag, below_tile, corner_real, corner_imag, rolled_probe, amplitude, tables):
    rows = SIDE // 8
    out_shape = (
        shape(rows, 3, 8, SIDE // 2),
        shape(rows, 3, 8, SIDE // 2),
        shape(2, SIDE, SIDE),
        shape(2, SIDE, SIDE),
        shape(2, 2, SIDE, SIDE),
    )
    return pl.pallas_call(
        visit_kernel,
        out_shape=out_shape,
        in_specs=[smem(), smem()] + [vmem()] * 9,
        out_specs=(vmem(),) * 5,
        scratch_shapes=[pltpu.VMEM(rolled_probe.shape, jnp.float32)],
        cost_estimate=pl.CostEstimate(flops=24 * 2 * 256**3 * 4, bytes_accessed=8 << 20, transcendentals=131072),
        compiler_params=pltpu.CompilerParams(vmem_limit_bytes=16 << 20),
    )(own, core, tile, right_real, right_imag, below_tile, corner_real, corner_imag, rolled_probe, amplitude, tables)


def fold_kernel(parts, copies):
    total = parts[...].sum(0)
    for k in range(copies.shape[0]):
        copies[k] = total


def fold(parts, count):
    return pl.pallas_call(
        fold_kernel,
        out_shape=shape(count, *parts.shape[1:]),
        in_specs=[vmem()],
        out_specs=vmem(),
        cost_estimate=pl.CostEstimate(flops=4000000000, bytes_accessed=1 << 19, transcendentals=0),
        compiler_params=pltpu.CompilerParams(vmem_limit_bytes=8 << 20),
    )(parts)


def settle_kernel(parts, corner, copies):
    total = parts[...].sum(0)
    new = [corner[part] + total[8 * part : 8 * part + 8] / (total[16:] + 1.0) for part in range(2)]
    both = jnp.concatenate(new, 0)
    for k in range(copies.shape[0]):
        copies[k] = both


def settle(parts, corner, count):
    return pl.pallas_call(
        settle_kernel,
        out_shape=shape(count, 16, SIDE // 2),
        in_specs=[vmem(), vmem()],
        out_specs=vmem(),
        cost_estimate=pl.CostEstimate(flops=100000, bytes_accessed=1 << 19, transcendentals=0),
        compiler_params=pltpu.CompilerParams(vmem_limit_bytes=8 << 20),
    )(parts, corner)


def body(positions, measured, object_field, probe):
    own = positions[0, 0]
    core = lax.axis_index("c")
    corner = lax.dynamic_slice(probe, (0, lax.axis_index(PLANE) * 8, core * (SIDE // 2)), (2, 8, SIDE // 2))
    right_real = passed_along(object_field[0], COL, -1)
    right_imag = passed_along(lax.optimization_barrier(object_field)[1], COL, -1)
    below_tile = passed_along(object_field, ROW, -1)
    rolled_probe = prepare(own, probe)
    right_real, rolled_probe, corner = lax.optimization_barrier((right_real, rolled_probe, corner))
    corner_real = passed_along(right_real, ROW, -1)
    corner_imag = passed_along(right_imag, ROW, -1)
    kept, sent, step_own, step_right, step_row = visit(
        own, core[None], object_field, right_real, right_imag, below_tile, corner_real, corner_imag, rolled_probe,
        measured[0, 0], jnp.asarray(dft_tables()),
    )
    other = lax.ppermute(sent, "c", [(0, 1), (1, 0)])
    rows = SIDE // 8
    pair = (kept + other).reshape(rows, 24, SIDE // 2)
    pair, step_row = lax.optimization_barrier((pair, step_row))
    summed = lax.all_to_all(pair, PLANE, 0, 0)
    step_row = passed_along(step_row, ROW, 1)
    summed = lax.all_to_all(fold(summed, lax.axis_size("y")), "y", 0, 0)
    step_right = passed_along(step_right + step_row[1], COL, 1)
    summed, step_row = lax.optimization_barrier((summed, step_row))
    near = lax.all_to_all(settle(summed, corner, rows), PLANE, 0, 0)
    new_object = finish(own, probe, object_field, step_own, step_row, step_right)
    near, new_object = lax.optimization_barrier((near, new_object))
    far = lax.ppermute(near, "c", [(0, 1), (1, 0)])
    pair = jnp.where(core == 0, jnp.stack([near, far]), jnp.stack([far, near]))
    new_probe = pair.reshape(2, rows, 2, 8, SIDE // 2).transpose(2, 1, 3, 0, 4).reshape(2, SIDE, SIDE)
    return (new_object, new_probe)


def solution(mesh):
    split = Mesh(mesh.devices.reshape(8, 2, 2, 2, 8), ROW + COL)
    in_specs = (P(ROW, COL), P(ROW, COL), P(None, ROW, COL), P())
    out_specs = (P(None, ROW, COL), P())
    return jax.shard_map(body, mesh=split, in_specs=in_specs, out_specs=out_specs, check_vma=False)
```

```python
import math

import jax
import jax.numpy as jnp
import ml_dtypes
import numpy as np
from jax import lax
from jax.experimental import pallas as pl
from jax.experimental.pallas import tpu as pltpu
from jax.sharding import Mesh
from jax.sharding import PartitionSpec as P

SIDE = 256
ROW = ("y", "xh", "c")
COL = ("xl", "z")
PLANE = ("xl", "xh", "z")


def passed_along(value, axis, steps):
    count = lax.axis_size(axis)
    leading, last = (max(0, -steps), min(count, count - steps))
    return lax.ppermute(value, axis, [(source, source + steps) for source in range(leading, last)])


def dft_tables():
    indices = np.arange(SIDE)
    angles = (indices[:, None] * indices[None, :] % SIDE) * (2.0 * math.pi / SIDE)
    cosine, sine = np.cos(angles) / math.sqrt(SIDE), np.sin(angles) / math.sqrt(SIDE)
    three = np.stack([cosine, sine, -sine])
    head = three.astype(ml_dtypes.bfloat16)
    rest = (three - head.astype(np.float64)).astype(ml_dtypes.bfloat16)
    return np.stack([head, rest], 1)


def halves(value):
    head = value.astype(jnp.bfloat16)
    return head, (value - head.astype(jnp.float32)).astype(jnp.bfloat16)


def dot(left, right):
    return jnp.dot(left, right, preferred_element_type=jnp.float32)


def block(tables, sign, which):
    up, down = (1, 2) if sign > 0 else (2, 1)
    upper = jnp.concatenate([tables[0, which], tables[up, which]], 1)
    return jnp.concatenate([upper, jnp.concatenate([tables[down, which], tables[0, which]], 1)], 0)


def apply_left(tables, sign, value):
    head, rest = halves(value)
    matrix = block(tables, sign, 0)
    return dot(matrix, head) + dot(matrix, rest) + dot(block(tables, sign, 1), head)


def apply_right(tables, sign, value):
    head, rest = halves(value)
    matrix = block(tables, sign, 0)
    return dot(head, matrix) + dot(rest, matrix) + dot(head, block(tables, sign, 1))


def to_columns(value):
    return jnp.concatenate(
        [jnp.concatenate([value[:SIDE, k * SIDE : (k + 1) * SIDE], value[SIDE:, k * SIDE : (k + 1) * SIDE]], 1) for k in range(2)], 0
    )


def rolled(value, rows, cols):
    return pltpu.roll(pltpu.roll(value, rows, 0), cols, 1)


def quadrants(row, col):
    below = lax.broadcasted_iota(jnp.int32, (SIDE, SIDE), 0) < row
    right = lax.broadcasted_iota(jnp.int32, (SIDE, SIDE), 1) < col
    return below, right


def prepare_kernel(own, probe, rolled_probe):
    for k in range(2):
        for part in range(2):
            rolled_probe[k, part] = rolled(probe[part], own[k, 0], own[k, 1])


def carried(block, first):
    line = lax.broadcasted_iota(jnp.int32, block.shape, 0)
    last = lax.broadcasted_iota(jnp.int32, block.shape, 1) == block.shape[1] - 1
    return [jnp.sum(jnp.where(last & (line == first + k), block, 0.0)).astype(jnp.int32) for k in range(4)]


def finish_kernel(own, probe, tile, step_own, step_row, step_right, new_tile):
    half = SIDE // 2
    intensity = probe[0] * probe[0] + probe[1] * probe[1]
    beside, above = step_right[0, :8, half:], step_row[1, 0, :8, half:]
    total = jnp.ones((SIDE, SIDE), jnp.float32)
    for spots, lies_below, lies_right in (
        ([own[k // 2, k % 2] for k in range(4)], False, False),
        (carried(beside, 4), False, True),
        (carried(above, 0), True, False),
        (carried(beside, 0), True, True),
    ):
        for k in range(2):
            row, col = spots[2 * k], spots[2 * k + 1]
            below, right = quadrants(row, col)
            inside = (below == lies_below) & (right == lies_right)
            total += jnp.where(inside, rolled(intensity, row, col), 0.0)
    last = lax.broadcasted_iota(jnp.int32, (SIDE, SIDE), 1) == SIDE - 1
    for part in range(2):
        arrived = step_row[0, part] + jnp.where(last, 0.0, step_right[part])
        new_tile[part] = tile[part] + (step_own[part] + arrived) / total


def visit_kernel(
    own, core, tile, right_real, right_imag, below_tile, corner_real, corner_imag, rolled_probe, amplitude,
    tables, kept, sent, step_own, step_right, step_row, patches,
):
    right_tile, corner_tile = (right_real, right_imag), (corner_real, corner_imag)
    exits = []
    for k in range(2):
        below, right = quadrants(own[k, 0], own[k, 1])
        for part in range(2):
            patches[k, part] = jnp.where(
                below,
                jnp.where(right, corner_tile[part][...], below_tile[part]),
                jnp.where(right, right_tile[part][...], tile[part]),
            )
        pr, pi = rolled_probe[k, 0], rolled_probe[k, 1]
        qr, qi = patches[k, 0], patches[k, 1]
        exits.append(jnp.concatenate([pr * qr - pi * qi, pr * qi + pi * qr], 0))
    exits = jnp.concatenate(exits, 1)
    field = to_columns(apply_left(tables, 1, exits))
    far = apply_right(tables, -1, field)
    far_real, far_imag = far[:, :SIDE], far[:, SIDE:]
    power = jnp.maximum(far_real * far_real + far_imag * far_imag, 0.25)
    factor = amplitude[...].reshape(2 * SIDE, SIDE).astype(jnp.float32) * lax.rsqrt(power) - 1.0
    change_real, change_imag = far_real * factor, far_imag * factor
    change = jnp.concatenate(
        [jnp.concatenate([change_real[k * SIDE : (k + 1) * SIDE], change_imag[k * SIDE : (k + 1) * SIDE]], 0) for k in range(2)], 1
    )
    chi = apply_right(tables, 1, to_columns(apply_left(tables, -1, change)))
    numerator = [jnp.zeros((SIDE, SIDE), jnp.float32)] * 3
    for k in range(2):
        chi_real = chi[k * SIDE : (k + 1) * SIDE, :SIDE]
        chi_imag = chi[k * SIDE : (k + 1) * SIDE, SIDE:]
        qr, qi = patches[k, 0], patches[k, 1]
        back_row, back_col = (SIDE - own[k, 0]) & (SIDE - 1), (SIDE - own[k, 1]) & (SIDE - 1)
        terms = (qr * chi_real + qi * chi_imag, qr * chi_imag - qi * chi_real, qr * qr + qi * qi)
        numerator = [total + rolled(term, back_row, back_col) for total, term in zip(numerator, terms)]
    first = core[0] == 0
    half = SIDE // 2
    for layer in range(3):
        one, other = numerator[layer][:, :half], numerator[layer][:, half:]
        kept[:, layer] = jnp.where(first, one, other).reshape(SIDE // 8, 8, half)
        sent[:, layer] = jnp.where(first, other, one).reshape(SIDE // 8, 8, half)
    line = lax.broadcasted_iota(jnp.int32, (8, half), 0)
    last = lax.broadcasted_iota(jnp.int32, (8, half), 1) == half - 1
    spots = jnp.zeros((8, half), jnp.int32)
    for k in range(4):
        spots = jnp.where((line & 3) == k, own[k // 2, k % 2], spots)
    spots = spots.astype(jnp.float32)

    def step(part, inside):
        total = jnp.zeros((SIDE, SIDE), jnp.float32)
        for k in range(2):
            chi_real = chi[k * SIDE : (k + 1) * SIDE, :SIDE]
            chi_imag = chi[k * SIDE : (k + 1) * SIDE, SIDE:]
            pr, pi = rolled_probe[k, 0], rolled_probe[k, 1]
            term = pr * chi_imag - pi * chi_real if part else pr * chi_real + pi * chi_imag
            total += jnp.where(inside(*quadrants(own[k, 0], own[k, 1])), term, 0.0)
        return total

    for part in range(2):
        step_row[0, part] = step(part, lambda below, right: below & jnp.logical_not(right))
        step_row[1, part] = step(part, lambda below, right: below & right)
    step_row[1, 0, :8, half:] = jnp.where(last & (line < 4), spots, step_row[1, 0, :8, half:])
    for part in range(2):
        step_right[part] = step(part, lambda below, right: right & jnp.logical_not(below))
        step_own[part] = step(part, lambda below, right: jnp.logical_not(below | right))
    step_right[0, :8, half:] = jnp.where(last & (line >= 4), spots, step_right[0, :8, half:])


def vmem():
    return pl.BlockSpec(memory_space=pltpu.VMEM)


def smem():
    return pl.BlockSpec(memory_space=pltpu.SMEM)


def shape(*sizes):
    return jax.ShapeDtypeStruct(sizes, jnp.float32)


def anywhere():
    return pl.BlockSpec(memory_space=pl.ANY)


def prepare(own, probe):
    return pl.pallas_call(
        prepare_kernel,
        out_shape=shape(2, 2, SIDE, SIDE),
        in_specs=[smem(), vmem()],
        out_specs=vmem(),
        cost_estimate=pl.CostEstimate(flops=2000000, bytes_accessed=2 << 20, transcendentals=0),
        compiler_params=pltpu.CompilerParams(vmem_limit_bytes=16 << 20),
    )(own, probe)


def finish(own, probe, tile, step_own, step_row, step_right):
    return pl.pallas_call(
        finish_kernel,
        out_shape=shape(2, SIDE, SIDE),
        in_specs=[smem()] + [vmem()] * 5,
        out_specs=vmem(),
        cost_estimate=pl.CostEstimate(flops=8000000, bytes_accessed=8 << 20, transcendentals=0),
        compiler_params=pltpu.CompilerParams(vmem_limit_bytes=16 << 20),
    )(own, probe, tile, step_own, step_row, step_right)


def visit(own, core, tile, right_real, right_imag, below_tile, corner_real, corner_imag, rolled_probe, amplitude, tables):
    rows = SIDE // 8
    out_shape = (
        shape(rows, 3, 8, SIDE // 2),
        shape(rows, 3, 8, SIDE // 2),
        shape(2, SIDE, SIDE),
        shape(2, SIDE, SIDE),
        shape(2, 2, SIDE, SIDE),
    )
    return pl.pallas_call(
        visit_kernel,
        out_shape=out_shape,
        in_specs=[smem(), smem()] + [vmem()] * 9,
        out_specs=(vmem(),) * 5,
        scratch_shapes=[pltpu.VMEM(rolled_probe.shape, jnp.float32)],
        cost_estimate=pl.CostEstimate(flops=24 * 2 * 256**3 * 4, bytes_accessed=8 << 20, transcendentals=131072),
        compiler_params=pltpu.CompilerParams(vmem_limit_bytes=16 << 20),
    )(own, core, tile, right_real, right_imag, below_tile, corner_real, corner_imag, rolled_probe, amplitude, tables)


def fold_kernel(parts, copies):
    total = parts[...].sum(0)
    for k in range(copies.shape[0]):
        copies[k] = total


def fold(parts, count):
    return pl.pallas_call(
        fold_kernel,
        out_shape=shape(count, *parts.shape[1:]),
        in_specs=[vmem()],
        out_specs=vmem(),
        cost_estimate=pl.CostEstimate(flops=100000000000, bytes_accessed=1 << 19, transcendentals=0),
        compiler_params=pltpu.CompilerParams(vmem_limit_bytes=8 << 20),
    )(parts)


def settle_kernel(parts, corner, copies):
    total = parts[...].sum(0)
    new = [corner[part] + total[8 * part : 8 * part + 8] / (total[16:] + 1.0) for part in range(2)]
    both = jnp.concatenate(new, 0)
    for k in range(copies.shape[0]):
        copies[k] = both


def settle(parts, corner, count):
    return pl.pallas_call(
        settle_kernel,
        out_shape=shape(count, 16, SIDE // 2),
        in_specs=[vmem(), vmem()],
        out_specs=vmem(),
        cost_estimate=pl.CostEstimate(flops=100000000000, bytes_accessed=1 << 19, transcendentals=0),
        compiler_params=pltpu.CompilerParams(vmem_limit_bytes=8 << 20),
    )(parts, corner)


def body(positions, measured, object_field, probe):
    own = positions[0, 0]
    core = lax.axis_index("c")
    corner = lax.dynamic_slice(probe, (0, lax.axis_index(PLANE) * 8, core * (SIDE // 2)), (2, 8, SIDE // 2))
    right_real = passed_along(object_field[0], COL, -1)
    right_imag = passed_along(lax.optimization_barrier(object_field)[1], COL, -1)
    below_tile = passed_along(object_field, ROW, -1)
    rolled_probe = prepare(own, probe)
    right_real, rolled_probe, corner = lax.optimization_barrier((right_real, rolled_probe, corner))
    corner_real = passed_along(right_real, ROW, -1)
    corner_imag = passed_along(right_imag, ROW, -1)
    kept, sent, step_own, step_right, step_row = visit(
        own, core[None], object_field, right_real, right_imag, below_tile, corner_real, corner_imag, rolled_probe,
        measured[0, 0], jnp.asarray(dft_tables()),
    )
    other = lax.ppermute(sent, "c", [(0, 1), (1, 0)])
    rows = SIDE // 8
    pair = (kept + other).reshape(rows, 24, SIDE // 2)
    pair, step_row = lax.optimization_barrier((pair, step_row))
    summed = lax.all_to_all(pair, PLANE, 0, 0)
    step_row = passed_along(step_row, ROW, 1)
    summed = lax.all_to_all(fold(summed, lax.axis_size("y")), "y", 0, 0)
    step_right = passed_along(step_right + step_row[1], COL, 1)
    summed, step_row = lax.optimization_barrier((summed, step_row))
    near = lax.all_to_all(settle(summed, corner, rows), PLANE, 0, 0)
    new_object = finish(own, probe, object_field, step_own, step_row, step_right)
    near, new_object = lax.optimization_barrier((near, new_object))
    far = lax.ppermute(near, "c", [(0, 1), (1, 0)])
    pair = jnp.where(core == 0, jnp.stack([near, far]), jnp.stack([far, near]))
    new_probe = pair.reshape(2, rows, 2, 8, SIDE // 2).transpose(2, 1, 3, 0, 4).reshape(2, SIDE, SIDE)
    return (new_object, new_probe)


def solution(mesh):
    split = Mesh(mesh.devices.reshape(8, 2, 2, 2, 8), ROW + COL)
    in_specs = (P(ROW, COL), P(ROW, COL), P(None, ROW, COL), P())
    out_specs = (P(None, ROW, COL), P())
    return jax.shard_map(body, mesh=split, in_specs=in_specs, out_specs=out_specs, check_vma=False)
```
